128 devices in a mesh: train: 16 (over y_hi, x, core), query: 8 (over y_lo, z).
Axes of the slice: x: 4, y: 4 (y_hi: 2, y_lo: 2; y = y_hi * 2 + y_lo), z: 4, core: 2. Of those that a mesh axis runs over, the one named last changes fastest.
Arguments:
- train_grads: bfloat16 [262144, 2048], P(('train', 'query')), may hold values from -128 to 128
- query_grads: bfloat16 [512, 2048], P(('train', 'query')), may hold values from -6 to 6
Outputs:
- scores: float32 [262144, 512], P(('train', 'query'))
- solved: float32 [512, 2048], P(('train', 'query'))
The draws below stay inside these ranges and needn't reach their ends.
All inputs are finite; a program needn't handle non-finite values.
Results may differ from the reference program's by a relative error of at most 0.0013.
The reference program's roundings to bfloat16 on the way count: a program that leaves them out, or rounds other values in their place, can miss the bound.
Values may be sent and summed in bfloat16 or wider, within the bound.
A program may use at most 64 MiB of HBM per device.

```python
import math
import jax
import jax.numpy as jnp
from jax import lax

FEATURES = 2048
ROWS_DEV = 2048
ITERS = 2
TRAIN_ROWS = 262144
QUERIES = 512
N_TRAIN = 16
N_QUERY = 8


def draw_train_grads(key, part):
    key = jax.random.fold_in(key, 7)
    key_base, key_cols, key_rows, key_mix = jax.random.split(key, 4)
    key_one, key_two, key_three = jax.random.split(key_mix, 3)
    total_rows = TRAIN_ROWS
    position = jnp.arange(total_rows, dtype=jnp.float32) / total_rows
    trend = 0.6 * jnp.exp(math.log(3.0) * position)
    base = jnp.clip(jax.random.normal(key_base, (total_rows, FEATURES), jnp.float32), -4.0, 4.0)
    columns = jnp.exp(jax.random.uniform(key_cols, (FEATURES,), jnp.float32, math.log(0.3), math.log(3.0)))
    spread = jnp.exp(jax.random.uniform(key_rows, (total_rows,), jnp.float32, math.log(0.5), math.log(2.0)))
    order_one = jax.random.permutation(key_one, FEATURES)
    order_two = jax.random.permutation(key_two, FEATURES)
    order_three = jax.random.permutation(key_three, FEATURES)
    others = jnp.take(base, order_one, axis=1) + jnp.take(base, order_two, axis=1)
    others = others + jnp.take(base, order_three, axis=1)
    mixed = (base + 0.6 * others) * (1.0 / math.sqrt(1.0 + 3.0 * 0.36))
    values = mixed * columns[None, :] * (spread * trend)[:, None]
    return values.astype(jnp.bfloat16)


def shard_levels(rng, dims, cuts, smallest, high):
    loudness = 1.0
    for axis_at, shards_of in cuts:
        steps = jax.random.uniform(jax.random.fold_in(jax.random.fold_in(rng, 6), axis_at), (shards_of,), jnp.float32, smallest / len(cuts), high / len(cuts))
        loudness = loudness * jnp.repeat(jnp.exp(steps), dims[axis_at] // shards_of).reshape((-1,) + (1,) * (len(dims) - 1 - axis_at))
    return loudness


def bell_draw(own_key, dims, scale, reach, cuts=(), kind=jnp.bfloat16):
    drawn = jax.random.normal(own_key, dims, jnp.float32) * scale
    if len(cuts) > 0:
        drawn = shard_levels(own_key, dims, cuts, -0.22, 0.18) * drawn
    return jnp.clip(drawn, min=-reach, max=reach).astype(kind)


def setup_inputs(seed: int = 0) -> dict:
    key_of = jax.random.split(jax.random.key(seed), 3)
    return {
        "train_grads": draw_train_grads(jax.random.fold_in(key_of[2], 71), 0),
        "query_grads": bell_draw(key_of[1], (QUERIES, FEATURES), 1.0, 6.0, ((0, 128),)),
    }


def rounded(state):
    low = state.astype(jnp.bfloat16)
    low = lax.optimization_barrier(low)
    return low.astype(jnp.float32)


def reference(train_grads, query_grads):
    devices = N_TRAIN * N_QUERY
    blocks = train_grads.reshape(devices, ROWS_DEV, FEATURES)

    def squares(carry, block):
        return carry + jnp.sum(jnp.square(block.astype(jnp.float32))), None

    total, _ = lax.scan(squares, jnp.float32(0.0), blocks)
    coef = FEATURES / (8.0 * total)
    query = query_grads.astype(jnp.float32)
    solved = query

    def curvature(state):
        low = rounded(state)

        def add(carry, block):
            grads = block.astype(jnp.float32)
            inner = jnp.dot(grads, low.T, precision=lax.Precision.HIGHEST)
            inner = rounded(inner)
            return carry + jnp.dot(inner.T, grads, precision=lax.Precision.HIGHEST), None

        result, _ = lax.scan(add, jnp.zeros((QUERIES, FEATURES), jnp.float32), blocks)
        return result

    for step in range(ITERS):
        solved = query + 0.99 * solved - coef * curvature(solved)
    low = rounded(solved)
    scale = 1.0 / (FEATURES ** 0.5)

    def score(block):
        return jnp.dot(block.astype(jnp.float32), low.T, precision=lax.Precision.HIGHEST) * scale

    scores = lax.map(score, blocks).reshape(TRAIN_ROWS, QUERIES)
    return scores, solved
```

```python
import functools

import jax
import jax.numpy as jnp
from jax import lax
from jax.experimental import pallas as pl
from jax.experimental.pallas import tpu as pltpu
from jax.sharding import PartitionSpec as P

ITERS = 2
MESH = pl.DeviceIdType.MESH
F32, BF16 = jnp.float32, jnp.bfloat16
ORDER = (0, 1, 3, 2)
TILE = 512


def div(a, b):
    return lax.div(a, jnp.int32(b))


def rem(a, b):
    return lax.rem(a, jnp.int32(b))


def nt(a, b):
    return lax.dot_general(a, b, (((1,), (1,)), ((), ())), preferred_element_type=F32)


def nn(a, b):
    return lax.dot_general(a, b, (((1,), (0,)), ((), ())), preferred_element_type=F32)


def wait_for(ref, sem):
    pltpu.make_async_copy(ref, ref, sem).wait()


def kernel(
    grads_ref, query_ref, scores_ref, solved_ref,
    grads, low, low_all, acc, inner, outgoing, arrived, scores,
    row_out, row_in, query, state, squares, square_out, squares_in,
    grads_sems, row_sems, gather_send, gather_recv, pair_send, pair_recv,
    reduce_send, reduce_recv, square_sems, out_sem,
):
    rows, width = grads_ref.shape
    quarter = width // 4
    half = low.shape[2]
    train, along = lax.axis_index("train"), lax.axis_index("query")
    core, x, y_hi = rem(train, 2), rem(div(train, 2), 4), div(train, 8)
    y_lo, z = div(along, 4), rem(along, 4)
    y = y_hi * 2 + y_lo

    def group_of(px, py):
        return (div(py, 2) * 4 + px) * 2 + rem(py, 2)

    def peer(at, dz):
        px, py, pz = rem(x + div(at, 4), 4), rem(y + rem(at, 4), 4), rem(z + dz, 4)
        return (div(py, 2) * 8 + px * 2 + core, rem(py, 2) * 4 + pz), group_of(px, py)

    blocks = arrived.at[0, pl.ds(1, 63)]
    sibling = (train + 1 - 2 * core, along)
    mine = group_of(x, y)
    mine_at = pl.multiple_of(mine * 16, 16)
    all_at = pl.multiple_of(div(mine, 2) * 64 + core * 32 + rem(mine, 2) * 16, 16)

    def remote(src, dst, send, recv, to):
        return pltpu.make_async_remote_copy(
            src_ref=src, dst_ref=dst, send_sem=send, recv_sem=recv, device_id=to, device_id_type=MESH
        )

    own_load = pltpu.make_async_copy(grads_ref, grads.at[pl.ds(0, rows)], grads_sems.at[0])
    own_load.start()

    barrier = pltpu.get_barrier_semaphore()
    pl.semaphore_signal(barrier, inc=1, device_id=sibling, device_id_type=MESH)

    def greet(n, carry):
        to, _ = peer(rem(n, 16), div(n, 16))
        pl.semaphore_signal(barrier, inc=1, device_id=to, device_id_type=MESH)
        return carry

    lax.fori_loop(1, 64, greet, 0)
    row_out[...] = jnp.zeros_like(row_out)
    for p in range(4):
        row_out[p, 0:4, :] = query_ref[:, p * quarter : (p + 1) * quarter].astype(F32)
    pl.semaphore_wait(barrier, 64)

    def exchange_rows(sems):
        for dz in range(1, 4):
            to, _ = peer(jnp.int32(0), dz)
            remote(row_out.at[rem(z + dz, 4)], row_in.at[z], sems.at[0], sems.at[1], to).start()
        row_in[z] = row_out[z]

    exchange_rows(row_sems.at[0])
    pair_load = remote(grads_ref, grads.at[pl.ds(rows, rows)], grads_sems.at[1], grads_sems.at[2], sibling)
    pair_load.start()
    wait_for(row_in.at[pl.ds(0, 3)], row_sems.at[0, 1])
    for p in range(4):
        query[p * 4 : p * 4 + 4, :] = row_in[p, 0:4, :]
    state[...] = query[...]
    wait_for(row_out.at[pl.ds(0, 3)], row_sems.at[0, 0])

    def gather(step, buffer, at):
        buffer[z, pl.ds(at, 16), :] = state[...].astype(BF16)
        block = buffer.at[z, pl.ds(at, 16)]
        for dz in ORDER:
            def send(n, carry, dz=dz):
                to, _ = peer(n, dz)
                remote(block, block, gather_send.at[step], gather_recv.at[step, dz], to).start()
                return carry

            lax.fori_loop(1 if dz == 0 else 0, 16, send, 0)

    def await_group(step, dz):
        taken = low.at[0, 0]
        wait_for(taken.at[pl.ds(0, 240)] if dz == 0 else taken, gather_recv.at[step, dz])

    def project(step, k, first, last):
        p = rem(z + 4 - ORDER[k], 4)
        columns = pl.ds(pl.multiple_of(p * quarter, quarter), quarter)

        @pl.loop(first // TILE, last // TILE)
        def _(i):
            here = pl.ds(pl.multiple_of(i * TILE, TILE), TILE)
            part = nt(low[step, p], grads[here, columns])
            if k == 0:
                acc[:, here] = part
            elif k < 3:
                acc[:, here] += part
            else:
                inner[:, here] = (acc[:, here] + part).astype(BF16)

    def reduce(step):
        @pl.loop(0, 4)
        def _(j):
            dz = rem(j + 1, 4)
            p = rem(z + dz, 4)
            columns = pl.ds(pl.multiple_of(p * quarter, quarter), quarter)
            outgoing[j] = nn(inner[...], grads[:, columns]).astype(BF16)

            def send(n, carry):
                @pl.when(n + dz > 0)
                def _():
                    to, group = peer(n, dz)
                    remote(
                        outgoing.at[j, pl.ds(pl.multiple_of(group * 16, 16), 16)],
                        arrived.at[step, dz * 16 + n],
                        reduce_send.at[step],
                        reduce_recv.at[step, dz],
                        to,
                    ).start()

                return carry

            lax.fori_loop(0, 16, send, 0)

        def add(first, last, total):
            return lax.fori_loop(first, last, lambda n, t: t + arrived[step, n].astype(F32), total)

        total = outgoing[3, pl.ds(mine_at, 16), :].astype(F32)
        for dz in (1, 2, 3):
            wait_for(arrived.at[step, pl.ds(dz * 16, 16)], reduce_recv.at[step, dz])
            total = add(dz * 16, dz * 16 + 16, total)
        wait_for(arrived.at[step, pl.ds(1, 15)], reduce_recv.at[step, 0])
        return add(1, 16, total)

    gather(0, low.at[0], mine_at)

    own_load.wait()

    def square(i, total):
        strip = pl.ds(pl.multiple_of(i * 256, 256), 256)
        part = jnp.zeros((256, 128), F32)
        for j in range(width // 128):
            value = grads[strip, j * 128 : (j + 1) * 128].astype(F32)
            part = part + value * value
        return total + jnp.sum(part.reshape(32, 8, 128), axis=0)

    own = lax.fori_loop(0, rows // 256, square, jnp.zeros((8, 128), F32))
    square_out[0] = jnp.sum(own, axis=0, keepdims=True)
    to_sibling = remote(square_out.at[0], square_out.at[1], square_sems.at[0], square_sems.at[1], sibling)
    to_sibling.start()
    to_sibling.wait()
    squares_in[0] = square_out[0] + square_out[1]

    def send_squares(n, carry):
        to, _ = peer(rem(n, 16), div(n, 16))
        remote(squares_in.at[0], squares_in.at[n], square_sems.at[2], square_sems.at[3], to).start()
        return carry

    lax.fori_loop(1, 64, send_squares, 0)

    for k in range(4):
        await_group(0, ORDER[k])
        project(0, k, 0, rows)
    pair_load.wait_recv()
    for k in range(4):
        project(0, k, rows, 2 * rows)

    coef = None
    for step in range(ITERS):
        if step > 0:
            for k in range(4):
                await_group(step, ORDER[k])
                project(step, k, 0, 2 * rows)
            wait_for(blocks, reduce_send.at[step - 1])
        curve = reduce(step)
        if step == 0:
            wait_for(squares_in.at[pl.ds(1, 63)], square_sems.at[3])
            coef = width / (8.0 * jnp.sum(squares_in[...]))
        state[...] = query[...] + 0.99 * state[...] - coef * curve
        if step < ITERS - 1:
            gather(step + 1, low.at[step + 1], mine_at)
        else:
            gather(step + 1, low_all, all_at)

    for p in range(4):
        row_out[p, 0:4, :] = state[p * 4 : p * 4 + 4, :]
    exchange_rows(row_sems.at[1])

    def strip_of(p, m):
        return low_all.at[p, pl.ds(pl.multiple_of(m * 64 + core * 32, 32), 32)]

    def score(k):
        p = rem(z + 4 - ORDER[k], 4)
        columns = pl.ds(pl.multiple_of(p * quarter, quarter), quarter)

        @pl.loop(0, rows // TILE)
        def _(i):
            here = pl.ds(pl.multiple_of(i * TILE, TILE), TILE)
            part = nt(grads[here, columns], low_all[p])
            if k == 0:
                scores[here, :] = part
            elif k < 3:
                scores[here, :] += part
            else:
                scores[here, :] = (scores[here, :] + part) * (1.0 / width**0.5)
                pltpu.make_async_copy(scores.at[here], scores_ref.at[here], out_sem).start()

    for k in range(5):
        if k < 4:
            await_group(ITERS, ORDER[k])
            p = rem(z + 4 - ORDER[k], 4)

            def pass_on(m, carry, p=p, k=k):
                strip = strip_of(p, m)
                remote(strip, strip, pair_send, pair_recv.at[k], sibling).start()
                return carry

            lax.fori_loop(0, 8, pass_on, 0)
        if k > 0:
            wait_for(low.at[0, 0], pair_recv.at[k - 1])
            score(k - 1)

    wait_for(row_in.at[pl.ds(0, 3)], row_sems.at[1, 1])
    for p in range(4):
        solved_ref[:, p * quarter : (p + 1) * quarter] = row_in[p, 0:4, :]

    wait_for(row_out.at[pl.ds(0, 3)], row_sems.at[1, 0])
    pair_load.wait_send()
    wait_for(squares_in.at[pl.ds(1, 63)], square_sems.at[2])
    wait_for(blocks, reduce_send.at[ITERS - 1])
    for step in range(ITERS + 1):
        wait_for(blocks, gather_send.at[step])
    wait_for(low.at[0], pair_send)
    wait_for(scores, out_sem)


def body(train_grads, query_grads):
    rows, width = train_grads.shape
    quarter = width // 4
    vmem, anywhere = pl.BlockSpec(memory_space=pltpu.VMEM), pl.BlockSpec(memory_space=pl.ANY)
    dma = pltpu.SemaphoreType.DMA
    return pl.pallas_call(
        kernel,
        out_shape=(
            jax.ShapeDtypeStruct((rows, 512), F32),
            jax.ShapeDtypeStruct((4, width), F32),
        ),
        in_specs=[anywhere, vmem],
        out_specs=(anywhere, vmem),
        scratch_shapes=[
            pltpu.VMEM((2 * rows, width), BF16),
            pltpu.VMEM((ITERS, 4, 256, quarter), BF16),
            pltpu.VMEM((4, 512, quarter), BF16),
            pltpu.VMEM((256, 2 * rows), F32),
            pltpu.VMEM((256, 2 * rows), BF16),
            pltpu.VMEM((4, 256, quarter), BF16),
            pltpu.VMEM((ITERS, 64, 16, quarter), BF16),
            pltpu.VMEM((rows, 512), F32),
            pltpu.VMEM((4, 8, quarter), F32),
            pltpu.VMEM((4, 8, quarter), F32),
            pltpu.VMEM((16, quarter), F32),
            pltpu.VMEM((16, quarter), F32),
            pltpu.VMEM((8, 128), F32),
            pltpu.VMEM((2, 1, 128), F32),
            pltpu.VMEM((64, 1, 128), F32),
            dma((3,)),
            dma((2, 2)),
            dma((ITERS + 1,)),
            dma((ITERS + 1, 4)),
            dma,
            dma((4,)),
            dma((ITERS,)),
            dma((ITERS, 4)),
            dma((4,)),
            dma,
        ],
        compiler_params=pltpu.CompilerParams(
            collective_id=0, has_side_effects=True, vmem_limit_bytes=56 * 2**20
        ),
        cost_estimate=pl.CostEstimate(
            flops=10 * rows * width * 512, bytes_accessed=4 * rows * width, transcendentals=0
        ),
    )(train_grads, query_grads)


def solution(mesh):
    placed = (P(("train", "query"), None), P(("train", "query"), None))
    return jax.shard_map(
        body,
        mesh=mesh,
        in_specs=placed,
        out_specs=placed,
        check_vma=False,
    )
```

```python
import functools

import jax
import jax.numpy as jnp
from jax import lax
from jax.experimental import pallas as pl
from jax.experimental.pallas import tpu as pltpu
from jax.sharding import PartitionSpec as P

ITERS = 2
MESH = pl.DeviceIdType.MESH
F32, BF16 = jnp.float32, jnp.bfloat16
ORDER = (1, 2, 3, 0)
AHEAD = 4


def div(a, b):
    return lax.div(a, jnp.int32(b))


def rem(a, b):
    return lax.rem(a, jnp.int32(b))


def nt(a, b):
    return lax.dot_general(a, b, (((1,), (1,)), ((), ())), preferred_element_type=F32)


def nn(a, b):
    return lax.dot_general(a, b, (((1,), (0,)), ((), ())), preferred_element_type=F32)


def far(i):
    return rem(2 + div(i * (i + 1), 2), 4)


def wait_for(ref, sem):
    pltpu.make_async_copy(ref, ref, sem).wait()


def kernel(
    grads_ref, query_ref, scores_ref, solved_ref,
    grads, low, low_all, acc, inner, outgoing, arrived,
    row_out, row_in, query, state, squares, square_out, squares_in,
    grads_sems, row_sems, gather_send, gather_recv, pair_send, pair_recv,
    reduce_send, reduce_recv, square_sems,
):
    rows, width = grads_ref.shape
    quarter = width // 4
    train, along = lax.axis_index("train"), lax.axis_index("query")
    core, x, y_hi = rem(train, 2), rem(div(train, 2), 4), div(train, 8)
    y_lo, z = div(along, 4), rem(along, 4)
    y = y_hi * 2 + y_lo

    def group_of(px, py):
        return (div(py, 2) * 4 + px) * 2 + rem(py, 2)

    def peer(at, dist):
        dx, dy = div(at, 4), rem(at, 4)
        px, py, pz = rem(x + dx, 4), rem(y + dy, 4), rem(z + dist + 8 - dx - dy, 4)
        return (div(py, 2) * 8 + px * 2 + core, rem(py, 2) * 4 + pz), group_of(px, py)

    blocks = arrived.at[0, pl.ds(1, 63)]
    spot = rem(x + y + z, 4)
    sibling = (train + 1 - 2 * core, along)
    mine = group_of(x, y)
    mine_at = pl.multiple_of(mine * 16, 16)
    all_at = pl.multiple_of(div(mine, 2) * 64 + core * 32 + rem(mine, 2) * 16, 16)

    def remote(src, dst, send, recv, to):
        return pltpu.make_async_remote_copy(
            src_ref=src, dst_ref=dst, send_sem=send, recv_sem=recv, device_id=to, device_id_type=MESH
        )

    own_load = pltpu.make_async_copy(grads_ref, grads.at[pl.ds(0, rows)], grads_sems.at[0])
    own_load.start()

    barrier = pltpu.get_barrier_semaphore()
    pl.semaphore_signal(barrier, inc=1, device_id=sibling, device_id_type=MESH)

    def greet(n, carry):
        to, _ = peer(rem(n, 16), div(n, 16))
        pl.semaphore_signal(barrier, inc=1, device_id=to, device_id_type=MESH)
        return carry

    lax.fori_loop(1, 64, greet, 0)
    row_out[...] = jnp.zeros_like(row_out)
    for p in range(4):
        row_out[p, 0:4, :] = query_ref[:, p * quarter : (p + 1) * quarter].astype(F32)
    pl.semaphore_wait(barrier, 64)

    def exchange_rows(first, slot, sems):
        for dz in range(1, 4):
            to, _ = peer(jnp.int32(0), dz)
            remote(row_out.at[rem(first + dz, 4)], row_in.at[slot], sems.at[0], sems.at[1], to).start()
        row_in[slot] = row_out[first]

    exchange_rows(spot, z, row_sems.at[0])
    pair_load = remote(grads_ref, grads.at[pl.ds(rows, rows)], grads_sems.at[1], grads_sems.at[2], sibling)
    pair_load.start()
    wait_for(row_in.at[pl.ds(0, 3)], row_sems.at[0, 1])
    for p in range(4):
        query[p * 4 : p * 4 + 4, :] = row_in[p, 0:4, :]
    state[...] = query[...]
    wait_for(row_out.at[pl.ds(0, 3)], row_sems.at[0, 0])

    def send_group(step, k, buffer, at):
        block = buffer.at[spot, pl.ds(at, 16)]

        def send(n, carry):
            to, _ = peer(far(div(n, 4)) * 4 + far(rem(n, 4)), ORDER[k])
            remote(block, block, gather_send.at[step, k], gather_recv.at[step, k], to).start()
            return carry

        lax.fori_loop(0, 15 if ORDER[k] == 0 else 16, send, 0)

    def gather(step, buffer, at):
        buffer[spot, pl.ds(at, 16), :] = state[...].astype(BF16)
        for k in range(AHEAD):
            send_group(step, k, buffer, at)

    def group_bytes(k):
        whole = low.at[0, 0]
        return whole.at[pl.ds(0, 240)] if ORDER[k] == 0 else whole

    def await_group(step, k, buffer, at):
        if k + AHEAD < 4:
            wait_for(group_bytes(k), gather_send.at[step, k])
            send_group(step, k + AHEAD, buffer, at)
        wait_for(group_bytes(k), gather_recv.at[step, k])

    def project(step, k):
        p = rem(spot + 4 - ORDER[k], 4)
        columns = pl.ds(pl.multiple_of(p * quarter, quarter), quarter)
        for part in range(2):
            here = slice(part * rows, (part + 1) * rows)
            value = nt(low[step, p], grads[here, columns])
            if k == 0:
                acc[:, here] = value
            elif k < 3:
                acc[:, here] += value
            else:
                inner[:, here] = (acc[:, here] + value).astype(BF16)

    def reduce(step):
        @pl.loop(0, 4)
        def _(j):
            dist = rem(j + 1, 4)
            p = rem(spot + dist, 4)
            columns = pl.ds(pl.multiple_of(p * quarter, quarter), quarter)
            outgoing[j] = nn(inner[...], grads[:, columns]).astype(BF16)

            def send(i, carry):
                n = far(div(i, 4)) * 4 + far(rem(i, 4))

                @pl.when(n + dist > 0)
                def _():
                    to, group = peer(n, dist)
                    remote(
                        outgoing.at[j, pl.ds(pl.multiple_of(group * 16, 16), 16)],
                        arrived.at[step, dist * 16 + n],
                        reduce_send.at[step],
                        reduce_recv.at[step, dist],
                        to,
                    ).start()

                return carry

            lax.fori_loop(0, 16, send, 0)

        def add(first, last, total):
            return lax.fori_loop(first, last, lambda n, t: t + arrived[step, n].astype(F32), total)

        total = outgoing[3, pl.ds(mine_at, 16), :].astype(F32)
        for dist in (1, 2, 3):
            wait_for(arrived.at[step, pl.ds(dist * 16, 16)], reduce_recv.at[step, dist])
            total = add(dist * 16, dist * 16 + 16, total)
        wait_for(arrived.at[step, pl.ds(1, 15)], reduce_recv.at[step, 0])
        return add(1, 16, total)

    gather(0, low.at[0], mine_at)

    own_load.wait()

    def square(i, total):
        strip = pl.ds(pl.multiple_of(i * 256, 256), 256)
        part = jnp.zeros((256, 128), F32)
        for j in range(width // 128):
            value = grads[strip, j * 128 : (j + 1) * 128].astype(F32)
            part = part + value * value
        return total + jnp.sum(part.reshape(32, 8, 128), axis=0)

    own = lax.fori_loop(0, rows // 256, square, jnp.zeros((8, 128), F32))
    square_out[0] = jnp.sum(own, axis=0, keepdims=True)
    to_sibling = remote(square_out.at[0], square_out.at[1], square_sems.at[0], square_sems.at[1], sibling)
    to_sibling.start()
    to_sibling.wait()
    squares_in[0] = square_out[0] + square_out[1]

    def send_squares(n, carry):
        to, _ = peer(rem(n, 16), div(n, 16))
        remote(squares_in.at[0], squares_in.at[n], square_sems.at[2], square_sems.at[3], to).start()
        return carry

    lax.fori_loop(1, 64, send_squares, 0)

    pair_load.wait_recv()

    coef = None
    for step in range(ITERS):
        for k in range(4):
            await_group(step, k, low.at[step], mine_at)
            project(step, k)
        if step > 0:
            wait_for(blocks, reduce_send.at[step - 1])
        curve = reduce(step)
        if step == 0:
            wait_for(squares_in.at[pl.ds(1, 63)], square_sems.at[3])
            coef = width / (8.0 * jnp.sum(squares_in[...]))
        state[...] = query[...] + 0.99 * state[...] - coef * curve
        if step < ITERS - 1:
            gather(step + 1, low.at[step + 1], mine_at)
        else:
            gather(step + 1, low_all, all_at)

    for p in range(4):
        row_out[p, 0:4, :] = state[p * 4 : p * 4 + 4, :]
    exchange_rows(z, spot, row_sems.at[1])

    def strip_of(p, m):
        return low_all.at[p, pl.ds(pl.multiple_of(m * 64 + core * 32, 32), 32)]

    def score(k):
        p = rem(spot + 4 - ORDER[k], 4)
        columns = pl.ds(pl.multiple_of(p * quarter, quarter), quarter)

        part = nt(grads[0:rows, columns], low_all[p])
        if k == 0:
            scores_ref[...] = part
        elif k < 3:
            scores_ref[...] += part
        else:
            scores_ref[...] = (scores_ref[...] + part) * (1.0 / width**0.5)

    for k in range(5):
        if k < 4:
            await_group(ITERS, k, low_all, all_at)
            p = rem(spot + 4 - ORDER[k], 4)

            def pass_on(m, carry, p=p, k=k):
                strip = strip_of(p, m)
                remote(strip, strip, pair_send, pair_recv.at[k], sibling).start()
                return carry

            lax.fori_loop(0, 8, pass_on, 0)
        if k > 0:
            wait_for(low.at[0, 0], pair_recv.at[k - 1])
            score(k - 1)

    wait_for(row_in.at[pl.ds(0, 3)], row_sems.at[1, 1])
    for p in range(4):
        solved_ref[:, p * quarter : (p + 1) * quarter] = row_in[p, 0:4, :]

    wait_for(row_out.at[pl.ds(0, 3)], row_sems.at[1, 0])
    pair_load.wait_send()
    wait_for(squares_in.at[pl.ds(1, 63)], square_sems.at[2])
    wait_for(blocks, reduce_send.at[ITERS - 1])
    for step in range(ITERS + 1):
        for k in range(4 - AHEAD, 4):
            wait_for(group_bytes(k), gather_send.at[step, k])
    wait_for(low.at[0], pair_send)


def body(train_grads, query_grads):
    rows, width = train_grads.shape
    quarter = width // 4
    vmem, anywhere = pl.BlockSpec(memory_space=pltpu.VMEM), pl.BlockSpec(memory_space=pl.ANY)
    dma = pltpu.SemaphoreType.DMA
    return pl.pallas_call(
        kernel,
        out_shape=(
            jax.ShapeDtypeStruct((rows, 512), F32),
            jax.ShapeDtypeStruct((4, width), F32),
        ),
        in_specs=[anywhere, vmem],
        out_specs=(vmem, vmem),
        scratch_shapes=[
            pltpu.VMEM((2 * rows, width), BF16),
            pltpu.VMEM((ITERS, 4, 256, quarter), BF16),
            pltpu.VMEM((4, 512, quarter), BF16),
            pltpu.VMEM((256, 2 * rows), F32),
            pltpu.VMEM((256, 2 * rows), BF16),
            pltpu.VMEM((4, 256, quarter), BF16),
            pltpu.VMEM((ITERS, 64, 16, quarter), BF16),
            pltpu.VMEM((4, 8, quarter), F32),
            pltpu.VMEM((4, 8, quarter), F32),
            pltpu.VMEM((16, quarter), F32),
            pltpu.VMEM((16, quarter), F32),
            pltpu.VMEM((8, 128), F32),
            pltpu.VMEM((2, 1, 128), F32),
            pltpu.VMEM((64, 1, 128), F32),
            dma((3,)),
            dma((2, 2)),
            dma((ITERS + 1, 4)),
            dma((ITERS + 1, 4)),
            dma,
            dma((4,)),
            dma((ITERS,)),
            dma((ITERS, 4)),
            dma((4,)),
            ],
        compiler_params=pltpu.CompilerParams(
            collective_id=0, has_side_effects=True, vmem_limit_bytes=44 * 2**20
        ),
        cost_estimate=pl.CostEstimate(
            flops=10 * rows * width * 512, bytes_accessed=4 * rows * width, transcendentals=0
        ),
    )(train_grads, query_grads)


def solution(mesh):
    placed = (P(("train", "query"), None), P(("train", "query"), None))
    return jax.shard_map(
        body,
        mesh=mesh,
        in_specs=placed,
        out_specs=placed,
        check_vma=False,
    )
```

```python
import functools

import jax
import jax.numpy as jnp
from jax import lax
from jax.experimental import pallas as pl
from jax.experimental.pallas import tpu as pltpu
from jax.sharding import PartitionSpec as P

ITERS = 2
MESH = pl.DeviceIdType.MESH
F32, BF16 = jnp.float32, jnp.bfloat16
ORDER = (1, 2, 3, 0)
AHEAD = 4


def div(a, b):
    return lax.div(a, jnp.int32(b))


def rem(a, b):
    return lax.rem(a, jnp.int32(b))


def nt(a, b):
    return lax.dot_general(a, b, (((1,), (1,)), ((), ())), preferred_element_type=F32)


def nn(a, b):
    return lax.dot_general(a, b, (((1,), (0,)), ((), ())), preferred_element_type=F32)


def far(i):
    return rem(2 + div(i * (i + 1), 2), 4)


def wait_for(ref, sem):
    pltpu.make_async_copy(ref, ref, sem).wait()


def kernel(
    grads_ref, query_ref, scores_ref, solved_ref,
    grads, low, low_all, acc, inner, outgoing, arrived,
    row_out, row_in, query, state, squares, square_out, squares_in,
    grads_sems, row_sems, gather_send, gather_recv, pair_send, pair_recv,
    reduce_send, reduce_recv, square_sems,
):
    rows, width = grads_ref.shape
    quarter = width // 4
    train, along = lax.axis_index("train"), lax.axis_index("query")
    core, x, y_hi = rem(train, 2), rem(div(train, 2), 4), div(train, 8)
    y_lo, z = div(along, 4), rem(along, 4)
    y = y_hi * 2 + y_lo

    def group_of(px, py):
        return (div(py, 2) * 4 + px) * 2 + rem(py, 2)

    def peer(at, dist):
        dx, dy = div(at, 4), rem(at, 4)
        px, py, pz = rem(x + dx, 4), rem(y + dy, 4), rem(z + dist + 8 - dx - dy, 4)
        return (div(py, 2) * 8 + px * 2 + core, rem(py, 2) * 4 + pz), group_of(px, py)

    blocks = arrived.at[0, pl.ds(1, 63)]
    spot = rem(x + y + z, 4)
    sibling = (train + 1 - 2 * core, along)
    mine = group_of(x, y)
    mine_at = pl.multiple_of(mine * 16, 16)
    all_at = pl.multiple_of(div(mine, 2) * 64 + core * 32 + rem(mine, 2) * 16, 16)

    def remote(src, dst, send, recv, to):
        return pltpu.make_async_remote_copy(
            src_ref=src, dst_ref=dst, send_sem=send, recv_sem=recv, device_id=to, device_id_type=MESH
        )

    own_load = pltpu.make_async_copy(grads_ref, grads.at[pl.ds(0, rows)], grads_sems.at[0])
    own_load.start()

    barrier = pltpu.get_barrier_semaphore()
    pl.semaphore_signal(barrier, inc=1, device_id=sibling, device_id_type=MESH)

    def greet(n, carry):
        to, _ = peer(rem(n, 16), div(n, 16))
        pl.semaphore_signal(barrier, inc=1, device_id=to, device_id_type=MESH)
        return carry

    lax.fori_loop(1, 64, greet, 0)
    row_out[...] = jnp.zeros_like(row_out)
    for p in range(4):
        row_out[p, 0:4, :] = query_ref[:, p * quarter : (p + 1) * quarter].astype(F32)
    own_load.wait()

    def square(i, total):
        strip = pl.ds(pl.multiple_of(i * 256, 256), 256)
        part = jnp.zeros((256, 128), F32)
        for j in range(width // 128):
            value = grads[strip, j * 128 : (j + 1) * 128].astype(F32)
            part = part + value * value
        return total + jnp.sum(part.reshape(32, 8, 128), axis=0)

    own = lax.fori_loop(0, rows // 256, square, jnp.zeros((8, 128), F32))
    pl.semaphore_wait(barrier, 64)

    def exchange_rows(first, slot, sems):
        for dz in range(1, 4):
            to, _ = peer(jnp.int32(0), dz)
            remote(row_out.at[rem(first + dz, 4)], row_in.at[slot], sems.at[0], sems.at[1], to).start()
        row_in[slot] = row_out[first]

    exchange_rows(spot, z, row_sems.at[0])
    pair_load = remote(grads_ref, grads.at[pl.ds(rows, rows)], grads_sems.at[1], grads_sems.at[2], sibling)
    pair_load.start()
    wait_for(row_in.at[pl.ds(0, 3)], row_sems.at[0, 1])
    for p in range(4):
        query[p * 4 : p * 4 + 4, :] = row_in[p, 0:4, :]
    state[...] = query[...]
    wait_for(row_out.at[pl.ds(0, 3)], row_sems.at[0, 0])

    def send_group(step, k, buffer, at):
        block = buffer.at[spot, pl.ds(at, 16)]

        def send(n, carry):
            to, _ = peer(far(div(n, 4)) * 4 + far(rem(n, 4)), ORDER[k])
            remote(block, block, gather_send.at[step, k], gather_recv.at[step, k], to).start()
            return carry

        lax.fori_loop(0, 15 if ORDER[k] == 0 else 16, send, 0)

    def gather(step, buffer, at):
        buffer[spot, pl.ds(at, 16), :] = state[...].astype(BF16)
        for k in range(AHEAD):
            send_group(step, k, buffer, at)

    def group_bytes(k):
        whole = low.at[0, 0]
        return whole.at[pl.ds(0, 240)] if ORDER[k] == 0 else whole

    def await_group(step, k, buffer, at):
        if k + AHEAD < 4:
            wait_for(group_bytes(k), gather_send.at[step, k])
            send_group(step, k + AHEAD, buffer, at)
        wait_for(group_bytes(k), gather_recv.at[step, k])

    def project(step, k):
        p = rem(spot + 4 - ORDER[k], 4)
        columns = pl.ds(pl.multiple_of(p * quarter, quarter), quarter)
        for part in range(2):
            here = slice(part * rows, (part + 1) * rows)
            value = nt(low[step, p], grads[here, columns])
            if k == 0:
                acc[:, here] = value
            elif k < 3:
                acc[:, here] += value
            else:
                inner[:, here] = (acc[:, here] + value).astype(BF16)

    def reduce(step):
        for j in range(4):
            dist = (j + 1) % 4
            p = rem(spot + dist, 4)
            columns = pl.ds(pl.multiple_of(p * quarter, quarter), quarter)
            outgoing[j] = nn(inner[...], grads[:, columns]).astype(BF16)

            def send(i, carry, j=j, dist=dist):
                n = far(div(i, 4)) * 4 + far(rem(i, 4))
                to, group = peer(n, dist)
                remote(
                    outgoing.at[j, pl.ds(pl.multiple_of(group * 16, 16), 16)],
                    arrived.at[step, dist * 16 + n],
                    reduce_send.at[step],
                    reduce_recv.at[step, dist],
                    to,
                ).start()
                return carry

            lax.fori_loop(0, 16 if dist else 15, send, 0)

        def add(first, last, total):
            return lax.fori_loop(first, last, lambda n, t: t + arrived[step, n].astype(F32), total)

        total = outgoing[3, pl.ds(mine_at, 16), :].astype(F32)
        for dist in (1, 2, 3):
            wait_for(arrived.at[step, pl.ds(dist * 16, 16)], reduce_recv.at[step, dist])
            total = add(dist * 16, dist * 16 + 16, total)
        wait_for(arrived.at[step, pl.ds(1, 15)], reduce_recv.at[step, 0])
        return add(1, 16, total)

    gather(0, low.at[0], mine_at)

    square_out[0] = jnp.sum(own, axis=0, keepdims=True)
    to_sibling = remote(square_out.at[0], square_out.at[1], square_sems.at[0], square_sems.at[1], sibling)
    to_sibling.start()
    to_sibling.wait()
    squares_in[0] = square_out[0] + square_out[1]

    def send_squares(n, carry):
        to, _ = peer(rem(n, 16), div(n, 16))
        remote(squares_in.at[0], squares_in.at[n], square_sems.at[2], square_sems.at[3], to).start()
        return carry

    lax.fori_loop(1, 64, send_squares, 0)

    pair_load.wait_recv()

    coef = None
    for step in range(ITERS):
        for k in range(4):
            await_group(step, k, low.at[step], mine_at)
            project(step, k)
        if step > 0:
            wait_for(blocks, reduce_send.at[step - 1])
        curve = reduce(step)
        if step == 0:
            wait_for(squares_in.at[pl.ds(1, 63)], square_sems.at[3])
            coef = width / (8.0 * jnp.sum(squares_in[...]))
        state[...] = query[...] + 0.99 * state[...] - coef * curve
        if step < ITERS - 1:
            gather(step + 1, low.at[step + 1], mine_at)
        else:
            gather(step + 1, low_all, all_at)

    for p in range(4):
        row_out[p, 0:4, :] = state[p * 4 : p * 4 + 4, :]
    exchange_rows(z, spot, row_sems.at[1])

    def strip_of(p, m):
        return low_all.at[p, pl.ds(pl.multiple_of(m * 64 + core * 32, 32), 32)]

    def score(k):
        p = rem(spot + 4 - ORDER[k], 4)
        columns = pl.ds(pl.multiple_of(p * quarter, quarter), quarter)

        part = nt(grads[0:rows, columns], low_all[p])
        if k == 0:
            scores_ref[...] = part
        elif k < 3:
            scores_ref[...] += part
        else:
            scores_ref[...] = (scores_ref[...] + part) * (1.0 / width**0.5)

    for k in range(5):
        if k < 4:
            await_group(ITERS, k, low_all, all_at)
            p = rem(spot + 4 - ORDER[k], 4)

            def pass_on(m, carry, p=p, k=k):
                strip = strip_of(p, m)
                remote(strip, strip, pair_send, pair_recv.at[k], sibling).start()
                return carry

            lax.fori_loop(0, 8, pass_on, 0)
        if k > 0:
            wait_for(low.at[0, 0], pair_recv.at[k - 1])
            score(k - 1)

    wait_for(row_in.at[pl.ds(0, 3)], row_sems.at[1, 1])
    for p in range(4):
        solved_ref[:, p * quarter : (p + 1) * quarter] = row_in[p, 0:4, :]

    wait_for(row_out.at[pl.ds(0, 3)], row_sems.at[1, 0])
    pair_load.wait_send()
    wait_for(squares_in.at[pl.ds(1, 63)], square_sems.at[2])
    wait_for(blocks, reduce_send.at[ITERS - 1])
    for step in range(ITERS + 1):
        for k in range(4 - AHEAD, 4):
            wait_for(group_bytes(k), gather_send.at[step, k])
    wait_for(low.at[0], pair_send)


def body(train_grads, query_grads):
    rows, width = train_grads.shape
    quarter = width // 4
    vmem, anywhere = pl.BlockSpec(memory_space=pltpu.VMEM), pl.BlockSpec(memory_space=pl.ANY)
    dma = pltpu.SemaphoreType.DMA
    return pl.pallas_call(
        kernel,
        out_shape=(
            jax.ShapeDtypeStruct((rows, 512), F32),
            jax.ShapeDtypeStruct((4, width), F32),
        ),
        in_specs=[anywhere, vmem],
        out_specs=(vmem, vmem),
        scratch_shapes=[
            pltpu.VMEM((2 * rows, width), BF16),
            pltpu.VMEM((ITERS, 4, 256, quarter), BF16),
            pltpu.VMEM((4, 512, quarter), BF16),
            pltpu.VMEM((256, 2 * rows), F32),
            pltpu.VMEM((256, 2 * rows), BF16),
            pltpu.VMEM((4, 256, quarter), BF16),
            pltpu.VMEM((ITERS, 64, 16, quarter), BF16),
            pltpu.VMEM((4, 8, quarter), F32),
            pltpu.VMEM((4, 8, quarter), F32),
            pltpu.VMEM((16, quarter), F32),
            pltpu.VMEM((16, quarter), F32),
            pltpu.VMEM((8, 128), F32),
            pltpu.VMEM((2, 1, 128), F32),
            pltpu.VMEM((64, 1, 128), F32),
            dma((3,)),
            dma((2, 2)),
            dma((ITERS + 1, 4)),
            dma((ITERS + 1, 4)),
            dma,
            dma((4,)),
            dma((ITERS,)),
            dma((ITERS, 4)),
            dma((4,)),
            ],
        compiler_params=pltpu.CompilerParams(
            collective_id=0, has_side_effects=True, vmem_limit_bytes=44 * 2**20
        ),
        cost_estimate=pl.CostEstimate(
            flops=10 * rows * width * 512, bytes_accessed=4 * rows * width, transcendentals=0
        ),
    )(train_grads, query_grads)


def solution(mesh):
    placed = (P(("train", "query"), None), P(("train", "query"), None))
    return jax.shard_map(
        body,
        mesh=mesh,
        in_specs=placed,
        out_specs=placed,
        check_vma=False,
    )
```
